512 devices in a mesh: dp: 64 (over x, z_lo, y), mp: 8 (over z_hi, core).
Axes of the slice: x: 4, y: 8, z: 8 (z_hi: 4, z_lo: 2; z = z_hi * 2 + z_lo), core: 2. Of those that a mesh axis runs over, the one named last changes fastest.
Arguments:
- query_states: bfloat16 [8192, 2048], P('dp'), may hold values from -6 to 6
- passage_states: bfloat16 [8192, 2048], P('dp'), may hold values from -6 to 6
- proj_weight: bfloat16 [2048, 2048], P('dp', 'mp'), may hold values from -0.125 to 0.125
- positive_index: int32 [8192], P('dp'), may hold values from 0 to 127
- logit_scale: float32 [1], replicated, may hold values from 0.01 to 0.04
- logit_bias: float32 [1], replicated, may hold values from -1.5 to 0.5
Outputs:
- grad_queries: float32 [8192, 2048], P('dp', 'mp')
- grad_passages: float32 [8192, 2048], P('dp', 'mp')
The draws below stay inside these ranges and needn't reach their ends.
All inputs are finite; a program needn't handle non-finite values.
Results may differ from the reference program's by a relative error of at most 0.011.
Values may be sent and summed in bfloat16 or wider, within the bound.
No kernel may reach another device: no remote copies, remote signals or barrier semaphores. Data moves between devices by JAX's collectives and lax.ppermute only.
A program may use at most 64 MiB of HBM per device.

```python
import math
import jax
import jax.numpy as jnp
from jax import lax

D = 2048
TOK_DEV = 128
TOKENS = 8192
N_MP = 8


def place_ends(entries, own_key, smallest, high):
    longest = entries.shape.index(max(entries.shape))
    spots = []
    for shift in (0, 1):
        where = [jax.random.randint(jax.random.fold_in(own_key, axis), (), 0, length) for axis, length in enumerate(entries.shape)]
        where[longest] = (where[longest] + shift) % entries.shape[longest]
        spots.append(tuple(where))
    return entries.at[spots[0]].set(smallest).at[spots[1]].set(high)


def levels(stream_key, shape, split, low, top_value):
    def one(axis_at, blocks):
        steps = jax.random.uniform(jax.random.fold_in(jax.random.fold_in(stream_key, 6), axis_at), (blocks,), jnp.float32, low / len(split), top_value / len(split))
        return jnp.repeat(jnp.exp(steps), shape[axis_at] // blocks).reshape((-1,) + (1,) * (len(shape) - axis_at - 1))

    gain = one(*split[0])
    for cut in split[1:]:
        gain = gain * one(*cut)
    return gain


def centred(own_key, extent, spread, limit, shards=(), kind=jnp.bfloat16):
    gain = levels(own_key, extent, shards, -0.22, 0.18) if shards else 1.0
    entries = jax.random.normal(own_key, extent, jnp.float32) * spread * gain
    return jnp.minimum(jnp.maximum(entries, -limit), limit).astype(kind)


def setup_inputs(seed: int = 0) -> dict:
    arg_keys = jax.random.split(jax.random.key(seed), 7)
    return {
        "query_states": centred(arg_keys[0], (TOKENS, D), 1.0, 6.0, ((0, 64),)),
        "passage_states": centred(arg_keys[1], (TOKENS, D), 1.0, 6.0, ((0, 64),)),
        "proj_weight": centred(arg_keys[2], (D, D), D ** -0.5, 0.125, ((0, 64), (1, 8))),
        "positive_index": place_ends(jax.random.randint(arg_keys[3], (TOKENS,), 0, TOK_DEV), jax.random.fold_in(arg_keys[3], 1), 0, TOK_DEV - 1).astype(jnp.int32),
        "logit_scale": jnp.clip(jnp.exp(jax.random.uniform(arg_keys[4], (1,), jnp.float32, math.log(0.01), math.log(0.04))), 0.01, 0.04),
        "logit_bias": jnp.clip(jax.random.uniform(arg_keys[5], (1,), jnp.float32, -1.5, 0.5), -1.5, 0.5),
    }


def reference(query_states, passage_states, proj_weight, positive_index, logit_scale, logit_bias):
    queries = jnp.dot(query_states, proj_weight, preferred_element_type=jnp.float32).astype(jnp.bfloat16)
    passages = jnp.dot(passage_states, proj_weight, preferred_element_type=jnp.float32).astype(jnp.bfloat16)
    scale_value = logit_scale[0]
    bias_value = logit_bias[0]
    block_count = TOKENS // TOK_DEV
    shard_width = D // N_MP
    passage_split = passages.astype(jnp.float32).reshape(TOKENS, N_MP, shard_width)
    column_ids = jnp.arange(TOKENS, dtype=jnp.int32)
    first_rows = jnp.arange(block_count, dtype=jnp.int32) * TOK_DEV

    def block_step(grad_p, inputs):
        query_block, position_block, first_row = inputs
        query_split = query_block.astype(jnp.float32).reshape(TOK_DEV, N_MP, shard_width)
        partial_value = jnp.einsum("imk,jmk->mij", query_split, passage_split)
        rounded = lax.optimization_barrier(partial_value.astype(jnp.bfloat16))
        scores = jnp.sum(rounded.astype(jnp.float32), axis=0)
        targets = (first_row + position_block).astype(jnp.int32)
        labels = (column_ids[None, :] == targets[:, None]).astype(jnp.float32)
        logits = scale_value * scores + bias_value
        weight = (jax.nn.sigmoid(logits) - labels).astype(jnp.bfloat16)
        grad_q = jnp.dot(weight, passages, preferred_element_type=jnp.float32)
        grad_p = grad_p + lax.dot_general(weight, query_block, (((0,), (0,)), ((), ())), preferred_element_type=jnp.float32)
        return grad_p, grad_q

    start_state = jnp.zeros((TOKENS, D), jnp.float32)
    inputs = (queries.reshape(block_count, TOK_DEV, D), positive_index.reshape(block_count, TOK_DEV), first_rows)
    grad_p, grad_q = lax.scan(block_step, start_state, inputs)
    grad_queries = scale_value * grad_q.reshape(TOKENS, D)
    grad_passages = scale_value * grad_p
    return (grad_queries, grad_passages)
```

```python
import jax
import jax.numpy as jnp
from jax import lax
from jax.sharding import Mesh, PartitionSpec as P

BF16 = jnp.bfloat16
F32 = jnp.float32
DP = ("x", "zl", "y")
MP = ("zh", "core")


def exchange(pieces, axes):
    return lax.all_to_all(pieces, axes, 0, 0, tiled=True)


def dot(left, right, contract):
    return lax.dot_general(left, right, (contract, ((), ())), preferred_element_type=F32)


def per_device(query_states, passage_states, proj_weight, positive_index, logit_scale, logit_bias):
    nx, nzl, ny, nzh = (lax.axis_size(a) for a in ("x", "zl", "y", "zh"))
    rows = query_states.shape[0]
    depth, cols = proj_weight.shape
    blocks = nzl * ny
    sub = rows // nzh
    scale_value = logit_scale[0]
    bias_value = logit_bias[0]

    w_all = exchange(jnp.broadcast_to(proj_weight[None], (nx * blocks, depth, cols)), DP)
    w_all = w_all.reshape(nx * blocks * depth, cols)
    passages = dot(passage_states, w_all, ((1,), (0,))).astype(BF16)
    queries = dot(query_states, w_all, ((1,), (0,))).astype(BF16)

    p_send = jnp.broadcast_to(passages.reshape(1, nzh, sub, cols), (blocks, nzh, sub, cols))
    p_tile = exchange(p_send.reshape(blocks * nzh, sub, cols), ("zl", "y", "zh"))
    p_tile = p_tile.reshape(blocks, nzh, sub, cols).transpose(0, 2, 1, 3)
    p_tile = p_tile.reshape(blocks * sub, nzh * cols)

    q_tile = exchange(jnp.broadcast_to(queries[None], (nzh, rows, cols)), "zh")
    q_tile = q_tile.transpose(1, 0, 2).reshape(rows, nzh * cols)
    q_tile = lax.all_gather(q_tile, "x", axis=0, tiled=True)

    part = dot(q_tile, p_tile, ((1,), (1,))).astype(BF16)
    other = lax.ppermute(part, "core", [(0, 1), (1, 0)])
    scores = part.astype(F32) + other.astype(F32)

    own_block = lax.axis_index("zl") * ny + lax.axis_index("y")
    place = positive_index - lax.axis_index("zh") * sub
    target = jnp.where((place >= 0) & (place < sub), own_block * sub + place, -1)
    own_x = jnp.arange(nx, dtype=jnp.int32)[:, None] == lax.axis_index("x")
    target = jnp.where(own_x, target[None, :], -1).reshape(nx * rows, 1)
    labels = (jnp.arange(blocks * sub, dtype=jnp.int32)[None, :] == target).astype(F32)
    logits = scale_value * scores + bias_value
    weight = (jax.nn.sigmoid(logits) - labels).astype(BF16)

    gp = dot(weight, q_tile, ((0,), (0,))).astype(BF16)
    gq = dot(weight, p_tile, ((1,), (0,))).astype(BF16)

    gp = gp.reshape(blocks, sub, nzh, cols).transpose(0, 2, 1, 3).reshape(blocks * nzh, sub, cols)
    gp = exchange(gp, ("zl", "y", "zh")).reshape(blocks, nzh, sub, cols)
    grad_p = jnp.sum(gp.astype(F32), axis=0).reshape(rows, cols)

    gq = exchange(gq, "x").reshape(nx, rows, nzh * cols)
    gq = jnp.sum(gq.astype(F32), axis=0).astype(BF16)
    gq = exchange(gq.reshape(rows, nzh, cols).transpose(1, 0, 2), "zh")
    grad_q = jnp.sum(gq.astype(F32), axis=0)
    return (scale_value * grad_q, scale_value * grad_p)


def solution(mesh):
    fine = Mesh(mesh.devices.reshape(4, 2, 8, 4, 2), DP + MP)
    in_specs = (P(DP, None), P(DP, None), P(DP, MP), P(DP), P(), P())
    out_specs = (P(DP, MP), P(DP, MP))
    return jax.shard_map(
        per_device, mesh=fine, in_specs=in_specs, out_specs=out_specs, check_vma=False
    )
```

```python
import jax
import jax.numpy as jnp
from jax import lax
from jax.sharding import Mesh, PartitionSpec as P

BF16 = jnp.bfloat16
F32 = jnp.float32
DP = ("x", "zl", "y")
MP = ("zh", "core")


def exchange(pieces, axes):
    return lax.all_to_all(pieces, axes, 0, 0, tiled=True)


def dot(left, right, contract):
    return lax.dot_general(left, right, (contract, ((), ())), preferred_element_type=F32)


def shifted(block, axis, step):
    size = lax.axis_size(axis)
    return lax.ppermute(block, axis, [(i, (i + step) % size) for i in range(size)])


def per_device(query_states, passage_states, proj_weight, positive_index, logit_scale, logit_bias):
    nx, nzl, ny, nzh = (lax.axis_size(a) for a in ("x", "zl", "y", "zh"))
    zh = lax.axis_index("zh")
    rows = query_states.shape[0]
    depth, cols = proj_weight.shape
    blocks = nzl * ny
    sub = rows // nzh
    scale_value = logit_scale[0]
    bias_value = logit_bias[0]

    w_all = exchange(jnp.broadcast_to(proj_weight[None], (nx * blocks, depth, cols)), DP)
    w_all = w_all.reshape(nx * blocks * depth, cols)
    passages = dot(passage_states, w_all, ((1,), (0,))).astype(BF16)
    queries = dot(query_states, w_all, ((1,), (0,))).astype(BF16)

    p_send = jnp.broadcast_to(passages.reshape(1, nzh, sub, cols), (blocks, nzh, sub, cols))
    p_tile = exchange(p_send.reshape(blocks * nzh, sub, cols), ("zl", "y", "zh"))
    p_tile = p_tile.reshape(blocks, nzh, sub, cols).transpose(0, 2, 1, 3)
    p_tile = p_tile.reshape(blocks * sub, nzh * cols)

    held = jnp.stack([queries] + [shifted(queries, "zh", k) for k in range(1, nzh)])
    ordered = [lax.dynamic_index_in_dim(held, (zh - j) % nzh, 0, False) for j in range(nzh)]
    q_own = jnp.concatenate(ordered, axis=1)
    q_tile = jnp.concatenate([q_own] + [shifted(q_own, "x", k) for k in range(1, nx)], axis=0)

    part = dot(q_tile, p_tile, ((1,), (1,))).astype(BF16)
    other = lax.ppermute(part, "core", [(0, 1), (1, 0)])
    scores = part.astype(F32) + other.astype(F32)

    own_block = lax.axis_index("zl") * ny + lax.axis_index("y")
    place = positive_index - zh * sub
    target = jnp.where((place >= 0) & (place < sub), own_block * sub + place, -1)
    target = jnp.pad(target, (0, (nx - 1) * rows), constant_values=-1)[:, None]
    labels = (jnp.arange(blocks * sub, dtype=jnp.int32)[None, :] == target).astype(F32)
    logits = scale_value * scores + bias_value
    weight = (jax.nn.sigmoid(logits) - labels).astype(BF16)

    gp = dot(weight, q_tile, ((0,), (0,))).astype(BF16)
    gp = gp.reshape(blocks, sub, nzh, cols).transpose(0, 2, 1, 3).reshape(blocks * nzh, sub, cols)
    gp = exchange(gp, ("zl", "y", "zh")).reshape(blocks, nzh, sub, cols)
    grad_p = jnp.sum(gp.astype(F32), axis=0).reshape(rows, cols)

    gq = dot(weight, p_tile, ((1,), (0,)))
    back = [
        shifted(gq[k * rows : (k + 1) * rows].astype(BF16), "x", -k).astype(F32)
        for k in range(1, nx)
    ]
    own = gq[:rows] + sum(back)

    def feature_block(j):
        return lax.dynamic_slice_in_dim(own, (j % nzh) * cols, cols, 1)

    grad_q = feature_block(zh) + sum(
        shifted(feature_block(zh + k).astype(BF16), "zh", k).astype(F32) for k in range(1, nzh)
    )
    return (scale_value * grad_q, scale_value * grad_p)


def solution(mesh):
    fine = Mesh(mesh.devices.reshape(4, 2, 8, 4, 2), DP + MP)
    in_specs = (P(DP, None), P(DP, None), P(DP, MP), P(DP), P(), P())
    out_specs = (P(DP, MP), P(DP, MP))
    return jax.shard_map(
        per_device, mesh=fine, in_specs=in_specs, out_specs=out_specs, check_vma=False
    )
```

```python
import jax
import jax.numpy as jnp
from jax import lax
from jax.sharding import Mesh, PartitionSpec as P

BF16 = jnp.bfloat16
F32 = jnp.float32
DP = ("x", "zl", "y")
MP = ("zh", "core")


def exchange(pieces, axes):
    return lax.all_to_all(pieces, axes, 0, 0, tiled=True)


def dot(left, right, contract):
    return lax.dot_general(left, right, (contract, ((), ())), preferred_element_type=F32)


def shifted(block, axis, step):
    size = lax.axis_size(axis)
    return lax.ppermute(block, axis, [(i, (i + step) % size) for i in range(size)])


def per_device(query_states, passage_states, proj_weight, positive_index, logit_scale, logit_bias):
    nx, nzl, ny, nzh = (lax.axis_size(a) for a in ("x", "zl", "y", "zh"))
    rows = query_states.shape[0]
    depth, cols = proj_weight.shape
    blocks = nzl * ny
    sub = rows // nzh
    scale_value = logit_scale[0]
    bias_value = logit_bias[0]

    w_part = exchange(jnp.broadcast_to(proj_weight[None], (blocks, depth, cols)), ("zl", "y"))
    w_part = w_part.reshape(1, blocks * depth, cols)
    w_all = exchange(jnp.broadcast_to(w_part, (nx, blocks * depth, cols)), "x")
    w_all = w_all.reshape(nx * blocks * depth, cols)
    passages = dot(passage_states, w_all, ((1,), (0,))).astype(BF16)
    queries = dot(query_states, w_all, ((1,), (0,))).astype(BF16)

    q_send = jnp.broadcast_to(queries[None], (nzh, rows, cols))
    own = jnp.concatenate([q_send, passages.reshape(nzh, sub, cols)], axis=1)
    own = exchange(own, "zh").transpose(1, 0, 2).reshape(rows + sub, nzh * cols)
    q_own, p_own = own[:rows], own[rows:]

    p_tile = exchange(jnp.broadcast_to(p_own[None], (blocks, sub, nzh * cols)), ("zl", "y"))
    p_tile = p_tile.reshape(blocks * sub, nzh * cols)
    q_tile = jnp.concatenate([q_own] + [shifted(q_own, "x", k) for k in range(1, nx)], axis=0)

    part = dot(q_tile, p_tile, ((1,), (1,))).astype(BF16)
    other = lax.ppermute(part, "core", [(0, 1), (1, 0)])
    scores = part.astype(F32) + other.astype(F32)

    own_block = lax.axis_index("zl") * ny + lax.axis_index("y")
    place = positive_index - lax.axis_index("zh") * sub
    target = jnp.where((place >= 0) & (place < sub), own_block * sub + place, -1)
    target = jnp.pad(target, (0, (nx - 1) * rows), constant_values=-1)[:, None]
    labels = (jnp.arange(blocks * sub, dtype=jnp.int32)[None, :] == target).astype(F32)
    logits = scale_value * scores + bias_value
    weight = (jax.nn.sigmoid(logits) - labels).astype(BF16)

    gp = dot(weight, q_tile, ((0,), (0,))).astype(BF16)
    gp = exchange(gp.reshape(blocks, sub, nzh * cols), ("zl", "y"))
    gp = jnp.sum(gp.astype(F32), axis=0)

    gq = dot(weight, p_tile, ((1,), (0,)))
    gq = gq[:rows] + sum(
        shifted(gq[k * rows : (k + 1) * rows].astype(BF16), "x", -k).astype(F32)
        for k in range(1, nx)
    )

    both = jnp.concatenate([gq, gp], axis=0).astype(BF16).reshape(rows + sub, nzh, cols)
    both = exchange(both.transpose(1, 0, 2), "zh").astype(F32)
    grad_q = jnp.sum(both[:, :rows], axis=0)
    grad_p = both[:, rows:].reshape(rows, cols)
    return (scale_value * grad_q, scale_value * grad_p)


def solution(mesh):
    fine = Mesh(mesh.devices.reshape(4, 2, 8, 4, 2), DP + MP)
    in_specs = (P(DP, None), P(DP, None), P(DP, MP), P(DP), P(), P())
    out_specs = (P(DP, MP), P(DP, MP))
    return jax.shard_map(
        per_device, mesh=fine, in_specs=in_specs, out_specs=out_specs, check_vma=False
    )
```

```python
import jax
import jax.numpy as jnp
from jax import lax
from jax.sharding import Mesh, PartitionSpec as P

BF16 = jnp.bfloat16
F32 = jnp.float32
DP = ("x", "zl", "y")
MP = ("zh", "core")


def exchange(pieces, axes):
    return lax.all_to_all(pieces, axes, 0, 0, tiled=True)


def dot(left, right, contract):
    return lax.dot_general(left, right, (contract, ((), ())), preferred_element_type=F32)


def shifted(block, axis, step):
    size = lax.axis_size(axis)
    return lax.ppermute(block, axis, [(i, (i + step) % size) for i in range(size)])


def per_device(query_states, passage_states, proj_weight, positive_index, logit_scale, logit_bias):
    nx, nzl, ny, nzh = (lax.axis_size(a) for a in ("x", "zl", "y", "zh"))
    rows = query_states.shape[0]
    depth, cols = proj_weight.shape
    blocks = nzl * ny
    sub = rows // nzh
    scale_value = logit_scale[0]
    bias_value = logit_bias[0]

    w_part = exchange(jnp.broadcast_to(proj_weight[None], (ny, depth, cols)), "y")
    w_part = w_part.reshape(1, ny * depth, cols)
    w_all = exchange(jnp.broadcast_to(w_part, (nx * nzl, ny * depth, cols)), ("x", "zl"))
    w_all = w_all.reshape(nx * blocks * depth, cols)
    passages = dot(passage_states, w_all, ((1,), (0,))).astype(BF16)
    queries = dot(query_states, w_all, ((1,), (0,))).astype(BF16)

    q_send = jnp.broadcast_to(queries[None], (nzh, rows, cols))
    own = jnp.concatenate([q_send, passages.reshape(nzh, sub, cols)], axis=1)
    own = exchange(own, "zh").transpose(1, 0, 2).reshape(rows + sub, nzh * cols)
    q_own, p_own = own[:rows], own[rows:]

    p_tile = exchange(jnp.broadcast_to(p_own[None], (blocks, sub, nzh * cols)), ("zl", "y"))
    p_tile = p_tile.reshape(blocks * sub, nzh * cols)
    q_tile = jnp.concatenate([q_own] + [shifted(q_own, "x", k) for k in range(1, nx)], axis=0)
    q_tile = lax.optimization_barrier(q_tile)

    part = dot(q_tile, p_tile, ((1,), (1,))).astype(BF16)
    other = lax.ppermute(part, "core", [(0, 1), (1, 0)])
    scores = part.astype(F32) + other.astype(F32)

    own_block = lax.axis_index("zl") * ny + lax.axis_index("y")
    place = positive_index - lax.axis_index("zh") * sub
    target = jnp.where((place >= 0) & (place < sub), own_block * sub + place, -1)
    target = jnp.pad(target, (0, (nx - 1) * rows), constant_values=-1)[:, None]
    labels = (jnp.arange(blocks * sub, dtype=jnp.int32)[None, :] == target).astype(F32)
    logits = scale_value * scores + bias_value
    weight = lax.optimization_barrier((jax.nn.sigmoid(logits) - labels).astype(BF16))

    gp = dot(weight, q_tile, ((0,), (0,))).astype(BF16)
    gp = exchange(gp.reshape(blocks, sub, nzh * cols), ("zl", "y"))
    gp = jnp.sum(gp.astype(F32), axis=0)

    gq = dot(weight, p_tile, ((1,), (0,)))
    gq = gq[:rows] + sum(
        shifted(gq[k * rows : (k + 1) * rows].astype(BF16), "x", -k).astype(F32)
        for k in range(1, nx)
    )

    both = jnp.concatenate([gq, gp], axis=0).astype(BF16).reshape(rows + sub, nzh, cols)
    both = exchange(both.transpose(1, 0, 2), "zh").astype(F32)
    grad_q = jnp.sum(both[:, :rows], axis=0)
    grad_p = both[:, rows:].reshape(rows, cols)
    return (scale_value * grad_q, scale_value * grad_p)


def solution(mesh):
    fine = Mesh(mesh.devices.reshape(4, 2, 8, 4, 2), DP + MP)
    in_specs = (P(DP, None), P(DP, None), P(DP, MP), P(DP), P(), P())
    out_specs = (P(DP, MP), P(DP, MP))
    return jax.shard_map(
        per_device, mesh=fine, in_specs=in_specs, out_specs=out_specs, check_vma=False
    )
```

```python
import jax
import jax.numpy as jnp
from jax import lax
from jax.sharding import Mesh, PartitionSpec as P

BF16 = jnp.bfloat16
F32 = jnp.float32
DP = ("x", "zl", "y")
MP = ("zh", "core")


def exchange(pieces, axes):
    return lax.all_to_all(pieces, axes, 0, 0, tiled=True)


def dot(left, right, contract):
    return lax.dot_general(left, right, (contract, ((), ())), preferred_element_type=F32)


def shifted(block, axis, step):
    size = lax.axis_size(axis)
    return lax.ppermute(block, axis, [(i, (i + step) % size) for i in range(size)])


def per_device(query_states, passage_states, proj_weight, positive_index, logit_scale, logit_bias):
    nx, nzl, ny, nzh = (lax.axis_size(a) for a in ("x", "zl", "y", "zh"))
    rows = query_states.shape[0]
    depth, cols = proj_weight.shape
    blocks = nzl * ny
    sub = rows // nzh
    scale_value = logit_scale[0]
    bias_value = logit_bias[0]

    w_part = exchange(jnp.broadcast_to(proj_weight[None], (ny, depth, cols)), "y")
    w_part = w_part.reshape(1, ny * depth, cols)
    w_all = exchange(jnp.broadcast_to(w_part, (nx * nzl, ny * depth, cols)), ("x", "zl"))
    w_all = w_all.reshape(nx * blocks * depth, cols)
    passages = dot(passage_states, w_all, ((1,), (0,))).astype(BF16)
    queries = dot(query_states, w_all, ((1,), (0,))).astype(BF16)

    q_send = jnp.broadcast_to(queries[None], (nzh, rows, cols))
    own = jnp.concatenate([q_send, passages.reshape(nzh, sub, cols)], axis=1)
    own = exchange(own, "zh")
    p_own = lax.optimization_barrier(own[:, rows:].transpose(1, 0, 2)).reshape(sub, nzh * cols)
    q_own = own[:, :rows].transpose(1, 0, 2).reshape(rows, nzh * cols)

    p_tile = exchange(jnp.broadcast_to(p_own[None], (blocks, sub, nzh * cols)), ("zl", "y"))
    p_tile = p_tile.reshape(blocks * sub, nzh * cols)
    q_tile = jnp.concatenate([q_own] + [shifted(q_own, "x", k) for k in range(1, nx)], axis=0)

    part = dot(p_tile, q_tile, ((1,), (1,))).astype(BF16)
    other = lax.ppermute(part, "core", [(0, 1), (1, 0)])
    scores = part.astype(F32) + other.astype(F32)

    own_block = lax.axis_index("zl") * ny + lax.axis_index("y")
    place = positive_index - lax.axis_index("zh") * sub
    target = jnp.where((place >= 0) & (place < sub), own_block * sub + place, -1)
    target = jnp.pad(target, (0, (nx - 1) * rows), constant_values=-1)[None, :]
    labels = (jnp.arange(blocks * sub, dtype=jnp.int32)[:, None] == target).astype(F32)
    logits = scale_value * scores + bias_value
    weight = lax.optimization_barrier((jax.nn.sigmoid(logits) - labels).astype(BF16))

    gp = dot(weight, q_tile, ((1,), (0,))).astype(BF16)
    gp = exchange(gp.reshape(blocks, sub, nzh * cols), ("zl", "y"))
    gp = jnp.sum(gp.astype(F32), axis=0)

    gq = dot(weight, p_tile, ((0,), (0,)))
    gq = gq[:rows] + sum(
        shifted(gq[k * rows : (k + 1) * rows].astype(BF16), "x", -k).astype(F32)
        for k in range(1, nx)
    )

    both = jnp.concatenate([gq, gp], axis=0).astype(BF16).reshape(rows + sub, nzh, cols)
    both = exchange(both.transpose(1, 0, 2), "zh").astype(F32)
    grad_q = jnp.sum(both[:, :rows], axis=0)
    grad_p = both[:, rows:].reshape(rows, cols)
    return (scale_value * grad_q, scale_value * grad_p)


def solution(mesh):
    fine = Mesh(mesh.devices.reshape(4, 2, 8, 4, 2), DP + MP)
    in_specs = (P(DP, None), P(DP, None), P(DP, MP), P(DP), P(), P())
    out_specs = (P(DP, MP), P(DP, MP))
    return jax.shard_map(
        per_device, mesh=fine, in_specs=in_specs, out_specs=out_specs, check_vma=False
    )
```

```python
import jax
import jax.numpy as jnp
from jax import lax
from jax.experimental import pallas as pl
from jax.experimental.pallas import tpu as pltpu
from jax.sharding import Mesh, PartitionSpec as P

BF16 = jnp.bfloat16
F32 = jnp.float32
DP = ("x", "zl", "y")
MP = ("zh", "core")


def exchange(pieces, axes):
    return lax.all_to_all(pieces, axes, 0, 0, tiled=True)


def dot(left, right, contract):
    return lax.dot_general(left, right, (contract, ((), ())), preferred_element_type=F32)


def shifted(block, axis, step):
    size = lax.axis_size(axis)
    return lax.ppermute(block, axis, [(i, (i + step) % size) for i in range(size)])


def finish_kernel(scale, both, grad_q, grad_p):
    rows = grad_q.shape[0]
    grad_q[...] = scale[0] * jnp.sum(both[:, :rows].astype(F32), axis=0)
    grad_p[...] = (scale[0] * both[:, rows:].astype(F32)).reshape(grad_p.shape)


def per_device(query_states, passage_states, proj_weight, positive_index, logit_scale, logit_bias):
    nx, nzl, ny, nzh = (lax.axis_size(a) for a in ("x", "zl", "y", "zh"))
    rows = query_states.shape[0]
    depth, cols = proj_weight.shape
    blocks = nzl * ny
    sub = rows // nzh
    scale_value = logit_scale[0]
    bias_value = logit_bias[0]

    w_part = exchange(jnp.broadcast_to(proj_weight[None], (ny, depth, cols)), "y")
    w_part = w_part.reshape(1, ny * depth, cols)
    w_all = exchange(jnp.broadcast_to(w_part, (nx * nzl, ny * depth, cols)), ("x", "zl"))
    w_all = w_all.reshape(nx * blocks * depth, cols)
    passages = dot(passage_states, w_all, ((1,), (0,))).astype(BF16)
    queries = dot(query_states, w_all, ((1,), (0,))).astype(BF16)

    q_send = jnp.broadcast_to(queries[None], (nzh, rows, cols))
    own = jnp.concatenate([q_send, passages.reshape(nzh, sub, cols)], axis=1)
    own = exchange(own, "zh")
    p_own = lax.optimization_barrier(own[:, rows:].transpose(1, 0, 2)).reshape(sub, nzh * cols)
    q_own = own[:, :rows].transpose(1, 0, 2).reshape(rows, nzh * cols)

    p_tile = exchange(jnp.broadcast_to(p_own[None], (blocks, sub, nzh * cols)), ("zl", "y"))
    p_tile = p_tile.reshape(blocks * sub, nzh * cols)
    q_tile = jnp.concatenate([q_own] + [shifted(q_own, "x", k) for k in range(1, nx)], axis=0)

    part = dot(p_tile, q_tile, ((1,), (1,))).astype(BF16)
    other = lax.ppermute(part, "core", [(0, 1), (1, 0)])
    scores = part.astype(F32) + other.astype(F32)

    own_block = lax.axis_index("zl") * ny + lax.axis_index("y")
    place = positive_index - lax.axis_index("zh") * sub
    target = jnp.where((place >= 0) & (place < sub), own_block * sub + place, -1)
    target = jnp.pad(target, (0, (nx - 1) * rows), constant_values=-1)[None, :]
    labels = (jnp.arange(blocks * sub, dtype=jnp.int32)[:, None] == target).astype(F32)
    logits = scale_value * scores + bias_value
    weight = lax.optimization_barrier((jax.nn.sigmoid(logits) - labels).astype(BF16))

    gp = dot(weight, q_tile, ((1,), (0,))).astype(BF16)
    gp = exchange(gp.reshape(blocks, sub, nzh * cols), ("zl", "y"))
    gp = jnp.sum(gp.astype(F32), axis=0)

    gq = dot(weight, p_tile, ((0,), (0,)))
    gq = gq[:rows] + sum(
        shifted(gq[k * rows : (k + 1) * rows].astype(BF16), "x", -k).astype(F32)
        for k in range(1, nx)
    )

    both = jnp.concatenate([gq, gp], axis=0).astype(BF16).reshape(rows + sub, nzh, cols)
    both = exchange(both.transpose(1, 0, 2), "zh")
    return pl.pallas_call(
        finish_kernel,
        in_specs=[
            pl.BlockSpec(memory_space=pltpu.SMEM),
            pl.BlockSpec(memory_space=pltpu.VMEM),
        ],
        out_shape=[jax.ShapeDtypeStruct((rows, cols), F32)] * 2,
        compiler_params=pltpu.CompilerParams(vmem_limit_bytes=8 * 1024 * 1024),
    )(logit_scale, both)


def solution(mesh):
    fine = Mesh(mesh.devices.reshape(4, 2, 8, 4, 2), DP + MP)
    in_specs = (P(DP, None), P(DP, None), P(DP, MP), P(DP), P(), P())
    out_specs = (P(DP, MP), P(DP, MP))
    return jax.shard_map(
        per_device, mesh=fine, in_specs=in_specs, out_specs=out_specs, check_vma=False
    )
```

```python
import jax
import jax.numpy as jnp
from jax import lax
from jax.experimental import pallas as pl
from jax.experimental.pallas import tpu as pltpu
from jax.sharding import Mesh, PartitionSpec as P

BF16 = jnp.bfloat16
F32 = jnp.float32
Y = ("yq", "yp")
DP = ("x", "zl") + Y
MP = ("zh", "core")


def exchange(pieces, axes):
    return lax.all_to_all(pieces, axes, 0, 0, tiled=True)


def dot(left, right, contract):
    return lax.dot_general(left, right, (contract, ((), ())), preferred_element_type=F32)


def shifted(block, axis, step):
    size = lax.axis_size(axis)
    return lax.ppermute(block, axis, [(i, (i + step) % size) for i in range(size)])


def finish_kernel(scale, both, grad_q, grad_p):
    rows = grad_q.shape[0]
    grad_q[...] = scale[0] * jnp.sum(both[:, :rows].astype(F32), axis=0)
    grad_p[...] = (scale[0] * both[:, rows:].astype(F32)).reshape(grad_p.shape)


def per_device(query_states, passage_states, proj_weight, positive_index, logit_scale, logit_bias):
    nx, nzl, ny, nzh = (lax.axis_size(a) for a in ("x", "zl", Y, "zh"))
    rows = query_states.shape[0]
    depth, cols = proj_weight.shape
    blocks = nzl * ny
    sub = rows // nzh
    scale_value = logit_scale[0]
    bias_value = logit_bias[0]

    nq, np = lax.axis_size("yq"), lax.axis_size("yp")
    w_part = exchange(jnp.broadcast_to(proj_weight[None], (nq, depth, cols)), "yq")
    w_part = jnp.broadcast_to(w_part[None], (nx * nzl * np, nq, depth, cols))
    w_all = exchange(w_part, ("x", "zl", "yp")).reshape(nx, nzl, np, nq, depth, cols)
    w_all = w_all.transpose(0, 1, 3, 2, 4, 5).reshape(nx * blocks * depth, cols)
    passages = dot(passage_states, w_all, ((1,), (0,))).astype(BF16)
    queries = dot(query_states, w_all, ((1,), (0,))).astype(BF16)

    q_send = jnp.broadcast_to(queries[None], (nzh, rows, cols))
    own = jnp.concatenate([q_send, passages.reshape(nzh, sub, cols)], axis=1)
    own = exchange(own, "zh")
    p_own = lax.optimization_barrier(own[:, rows:].transpose(1, 0, 2)).reshape(sub, nzh * cols)
    q_own = own[:, :rows].transpose(1, 0, 2).reshape(rows, nzh * cols)

    p_tile = exchange(jnp.broadcast_to(p_own[None], (blocks, sub, nzh * cols)), ("zl",) + Y)
    p_tile = p_tile.reshape(blocks * sub, nzh * cols)
    q_tile = jnp.concatenate([q_own] + [shifted(q_own, "x", k) for k in range(1, nx)], axis=0)

    part = dot(p_tile, q_tile, ((1,), (1,))).astype(BF16)
    other = lax.ppermute(part, "core", [(0, 1), (1, 0)])
    scores = part.astype(F32) + other.astype(F32)

    own_block = lax.axis_index("zl") * ny + lax.axis_index(Y)
    place = positive_index - lax.axis_index("zh") * sub
    target = jnp.where((place >= 0) & (place < sub), own_block * sub + place, -1)
    target = jnp.pad(target, (0, (nx - 1) * rows), constant_values=-1)[None, :]
    labels = (jnp.arange(blocks * sub, dtype=jnp.int32)[:, None] == target).astype(F32)
    logits = scale_value * scores + bias_value
    weight = lax.optimization_barrier((jax.nn.sigmoid(logits) - labels).astype(BF16))

    gp = dot(weight, q_tile, ((1,), (0,))).astype(BF16)
    gp = exchange(gp.reshape(blocks, sub, nzh * cols), ("zl",) + Y)
    gp = jnp.sum(gp.astype(F32), axis=0)

    gq = dot(weight, p_tile, ((0,), (0,)))
    gq = gq[:rows] + sum(
        shifted(gq[k * rows : (k + 1) * rows].astype(BF16), "x", -k).astype(F32)
        for k in range(1, nx)
    )

    both = jnp.concatenate([gq, gp], axis=0).astype(BF16).reshape(rows + sub, nzh, cols)
    both = exchange(both.transpose(1, 0, 2), "zh")
    return pl.pallas_call(
        finish_kernel,
        in_specs=[
            pl.BlockSpec(memory_space=pltpu.SMEM),
            pl.BlockSpec(memory_space=pltpu.VMEM),
        ],
        out_shape=[jax.ShapeDtypeStruct((rows, cols), F32)] * 2,
        compiler_params=pltpu.CompilerParams(vmem_limit_bytes=8 * 1024 * 1024),
    )(logit_scale, both)


def solution(mesh):
    fine = Mesh(mesh.devices.reshape(4, 2, 4, 2, 4, 2), DP + MP)
    in_specs = (P(DP, None), P(DP, None), P(DP, MP), P(DP), P(), P())
    out_specs = (P(DP, MP), P(DP, MP))
    return jax.shard_map(
        per_device, mesh=fine, in_specs=in_specs, out_specs=out_specs, check_vma=False
    )
```
